256 devices in a mesh: dp: 16 (over y_hi, z), ctx: 16 (over y_lo, x, core).
Axes of the slice: x: 4, y: 4 (y_hi: 2, y_lo: 2; y = y_hi * 2 + y_lo), z: 8, core: 2. Of those that a mesh axis runs over, the one named last changes fastest.
Arguments:
- queries: bfloat16 [49152, 4096], P(('dp', 'ctx')), may hold values from -140 to 140
- keys: bfloat16 [49152, 512], P(('dp', 'ctx')), may hold values from -5 to 5
- values: bfloat16 [49152, 512], P(('dp', 'ctx')), may hold values from -6 to 6
- block_order: int32 [16, 16], P('dp'), may hold values from 0 to 15, each once within a row
- query_maps: float32 [32, 128, 64], P('ctx'), may hold values from -0.5 to 0.5
- key_maps: float32 [32, 128, 64], P('ctx'), may hold values from -0.5 to 0.5
Outputs:
- teacher_out: bfloat16 [49152, 4096], P(('dp', 'ctx'))
- query_grads: float32 [32, 128, 64], P('ctx')
- key_grads: float32 [32, 128, 64], P('ctx')
The draws below stay inside these ranges and needn't reach their ends.
Inputs may be any that keep to these rules, and one draw needn't show every extreme that they name: Each row of block_order names every block once.
All inputs are finite; a program needn't handle non-finite values.
Results may differ from the reference program's by a relative error of at most 0.005.
Values may be sent and summed in bfloat16 or wider, within the bound.
No kernel may reach another device: no remote copies, remote signals or barrier semaphores. Data moves between devices by JAX's collectives and lax.ppermute only.
A program may use at most 128 MiB of HBM per device.

```python
import jax
import jax.numpy as jnp
from jax import lax

H = 32
KVH = 4
HD = 128
FH = 64
SPAN = 256
TOK_DEV = 192
SEQ = 3072
SEQS = 16
TOKENS = 49152
GROUP = 8
N_CTX = 16


def shared_keys(key):
    return jnp.clip(jax.random.normal(key, (TOKENS, KVH * HD), jnp.float32), -5.0, 5.0)


def draw_queries(key, part):
    key = jax.random.fold_in(key, 1)
    query_values = 2.0 * jnp.clip(jax.random.normal(key, (TOKENS, H * HD), jnp.float32), -5.0, 5.0)
    return query_values.astype(jnp.bfloat16)


def draw_keys(key, part):
    key_base = shared_keys(key)
    return key_base.astype(jnp.bfloat16)


def block_scale(own_key, dims, cuts, low, largest):
    loudness = 1.0
    for dim, blocks in cuts:
        steps = jax.random.uniform(jax.random.fold_in(jax.random.fold_in(own_key, 6), dim), (blocks,), jnp.float32, low / len(cuts), largest / len(cuts))
        loudness = loudness * jnp.repeat(jnp.exp(steps), dims[dim] // blocks).reshape((-1,) + (1,) * (len(dims) - 1 - dim))
    return loudness


def gaussian(rng, extent, deviation, most, cuts=(), kind=jnp.bfloat16):
    result = jax.random.normal(rng, extent, jnp.float32) * deviation
    if len(cuts) > 0:
        result = block_scale(rng, extent, cuts, -0.22, 0.18) * result
    return jnp.clip(result, min=-most, max=most).astype(kind)


def setup_inputs(seed: int = 0) -> dict:
    key_of = jax.random.split(jax.random.key(seed), 7)
    return {
        "queries": draw_queries(jax.random.fold_in(key_of[6], 71), 0),
        "keys": draw_keys(jax.random.fold_in(key_of[6], 71), 0),
        "values": gaussian(key_of[2], (TOKENS, KVH * HD), 1.0, 6.0, ((0, 256),)),
        "block_order": jax.vmap(lambda own: jax.random.permutation(own, N_CTX))(jax.random.split(key_of[3], SEQS)).reshape((SEQS, N_CTX)).astype(jnp.int32),
        "query_maps": gaussian(key_of[4], (H, HD, FH), HD ** -0.5, 0.5, ((0, 16),), jnp.float32),
        "key_maps": gaussian(key_of[5], (H, HD, FH), HD ** -0.5, 0.5, ((0, 16),), jnp.float32),
    }


HIGHEST = lax.Precision.HIGHEST

def features(inputs, weights):
    logits = jnp.dot(inputs.astype(jnp.float32), weights, precision=HIGHEST)
    return jnp.concatenate([jax.nn.softmax(logits, axis=-1), jax.nn.softmax(-logits, axis=-1)], axis=-1)

def student_loss(query_map, key_map, query_head, key_head, value_head, target_head, loss_scale):
    query_feats = features(query_head, query_map)
    key_feats = features(key_head, key_map)
    length = query_head.shape[0]
    span_count = length // SPAN
    feat_width = query_feats.shape[1]
    head_dim = value_head.shape[1]
    query_blocks = query_feats.reshape(span_count, SPAN, feat_width)
    key_blocks = key_feats.reshape(span_count, SPAN, feat_width)
    value_blocks = value_head.astype(jnp.float32).reshape(span_count, SPAN, head_dim)
    lower_mask = jnp.tril(jnp.ones((SPAN, SPAN), jnp.float32))

    def advance(state_pair, block_data):
        state, normal_sum = state_pair
        query_rows, key_rows, value_rows = block_data
        within = jnp.dot(query_rows, key_rows.T, precision=HIGHEST) * lower_mask
        numerator = jnp.dot(within, value_rows, precision=HIGHEST) + jnp.dot(query_rows, state, precision=HIGHEST)
        denominator = lax.optimization_barrier(jnp.sum(within, axis=1)) + jnp.dot(query_rows, normal_sum, precision=HIGHEST)
        updated = (state + jnp.dot(key_rows.T, value_rows, precision=HIGHEST), normal_sum + lax.optimization_barrier(jnp.sum(key_rows, axis=0)))
        return (updated, numerator / denominator[:, None])
    initial = (jnp.zeros((feat_width, head_dim), jnp.float32), jnp.zeros((feat_width,), jnp.float32))
    unused_state, outputs = lax.scan(advance, initial, (query_blocks, key_blocks, value_blocks))
    mismatch = outputs.reshape(length, head_dim) - target_head.astype(jnp.float32)
    return jnp.sum(mismatch * mismatch) * loss_scale

def teacher_sequence(seq_queries, seq_keys, seq_values, positions):
    query_heads = seq_queries.reshape(SEQ, H, HD).transpose(1, 0, 2)
    key_heads = seq_keys.reshape(SEQ, KVH, HD).transpose(1, 0, 2)
    value_heads = seq_values.reshape(SEQ, KVH, HD).transpose(1, 0, 2)
    causal_mask = positions[None, :] <= positions[:, None]

    def one_head(head_index):
        query_rows = query_heads[head_index]
        key_rows = key_heads[head_index // GROUP]
        value_rows = value_heads[head_index // GROUP]
        scores = jnp.dot(query_rows, key_rows.T, preferred_element_type=jnp.float32) * HD ** (-0.5)
        scores = jnp.where(causal_mask, scores, -1e+30)
        row_max = lax.optimization_barrier(jnp.max(scores, axis=-1, keepdims=True))
        weights = jnp.where(causal_mask, jnp.exp(scores - row_max), 0.0)
        numerator = jnp.dot(weights.astype(jnp.bfloat16), value_rows, preferred_element_type=jnp.float32)
        return (numerator / lax.optimization_barrier(jnp.sum(weights, axis=-1, keepdims=True))).astype(jnp.bfloat16)
    outputs = lax.map(one_head, jnp.arange(H, dtype=jnp.int32))
    return outputs.transpose(1, 0, 2).reshape(SEQ, H * HD)

def reference(queries, keys, values, block_order, query_maps, key_maps):
    local_rows = jnp.arange(SEQ, dtype=jnp.int32)

    def one_sequence(seq_index):
        start_row = (seq_index * SEQ).astype(jnp.int32)
        seq_queries = lax.dynamic_slice_in_dim(queries, start_row, SEQ, 0)
        seq_keys = lax.dynamic_slice_in_dim(keys, start_row, SEQ, 0)
        seq_values = lax.dynamic_slice_in_dim(values, start_row, SEQ, 0)
        seq_table = block_order[seq_index]
        positions = (seq_table[local_rows // TOK_DEV] * TOK_DEV + local_rows % TOK_DEV).astype(jnp.int32)
        teacher = teacher_sequence(seq_queries, seq_keys, seq_values, positions)

        def ordered(stored):
            return jnp.zeros_like(stored).at[positions].set(stored)
        query_heads = ordered(seq_queries).reshape(SEQ, H, HD).transpose(1, 0, 2)
        key_heads = ordered(seq_keys).reshape(SEQ, KVH, HD).transpose(1, 0, 2)
        value_heads = ordered(seq_values).reshape(SEQ, KVH, HD).transpose(1, 0, 2)
        target_heads = ordered(teacher).reshape(SEQ, H, HD).transpose(1, 0, 2)

        def head_grads(head_index):
            return jax.grad(student_loss, argnums=(0, 1))(query_maps[head_index], key_maps[head_index], query_heads[head_index], key_heads[head_index // GROUP], value_heads[head_index // GROUP], target_heads[head_index], 1.0 / SEQS)
        grads_query, grads_key = lax.map(head_grads, jnp.arange(H, dtype=jnp.int32))
        return (teacher, grads_query, grads_key)
    teachers, grads_query, grads_key = lax.map(one_sequence, jnp.arange(SEQS, dtype=jnp.int32))
    return (teachers.reshape(TOKENS, H * HD), lax.optimization_barrier(jnp.sum(grads_query, axis=0)), lax.optimization_barrier(jnp.sum(grads_key, axis=0)))
```

```python
import functools
import math

import jax
import jax.numpy as jnp
import numpy as np
from jax import lax
from jax.experimental import pallas as pl
from jax.experimental.pallas import tpu as pltpu
from jax.sharding import PartitionSpec as P

BF = jnp.bfloat16
F32 = jnp.float32
CHUNK = 256


def mm(a, b, ca=1, cb=0):
    return lax.dot_general(a, b, (((ca,), (cb,)), ((), ())), preferred_element_type=F32)


def split(x):
    high = x.astype(BF)
    return high, (x - high.astype(F32)).astype(BF)


def lower_mask():
    rows = lax.broadcasted_iota(jnp.int32, (CHUNK, CHUNK), 0)
    cols = lax.broadcasted_iota(jnp.int32, (CHUNK, CHUNK), 1)
    return cols <= rows


def teacher_kernel(scale, place, q_ref, k_ref, v_ref, o_ref, qs, ks, vs, os, scores, probs):
    blocks, rows, width = k_ref.shape
    tiles = blocks * rows // CHUNK
    for p in range(blocks):
        b = place[p]
        span = pl.ds(p * rows, rows)
        qs[span, :] = q_ref[b]
        ks[span, :] = k_ref[b]
        vs[span, :width] = v_ref[b]
    vs[:, width:] = jnp.ones((blocks * rows, width), BF)
    mask = lower_mask()
    tops = {}

    def first(i, j):
        s = mm(qs[pl.ds(i * CHUNK, CHUNK), :], ks[pl.ds(j * CHUNK, CHUNK), :], 1, 1)
        if i == j:
            s = jnp.where(mask, s, -1e30)
        scores[i % 2, j] = s
        top = functools.reduce(
            jnp.maximum, [s[:, g * width : (g + 1) * width] for g in range(CHUNK // width)]
        )
        tops[i] = top if j == 0 else jnp.maximum(tops[i], top)

    def second(i, j, peak):
        p = jnp.exp2((scores[i % 2, j] - peak) * scale)
        probs[i % 2, :, j * CHUNK : (j + 1) * CHUNK] = p.astype(BF)

    def finish(i):
        keys = (i + 1) * CHUNK
        both = mm(probs[i % 2, :, :keys], vs[:keys, :])
        os[pl.ds(i * CHUNK, CHUNK), :] = (both[:, :width] / both[:, width:]).astype(BF)

    for i in range(tiles + 1):
        if i > 0:
            peak = jnp.max(tops[i - 1], axis=1, keepdims=True)
        for j in range(i + 1):
            if i < tiles:
                first(i, j)
            if i > 0 and j < i:
                second(i - 1, j, peak)
        if i > 0:
            finish(i - 1)
    for p in range(blocks):
        o_ref[place[p]] = os[pl.ds(p * rows, rows), :]


def teacher(place, q, k, v):
    blocks, rows, width = k.shape
    n = blocks * rows
    tiles = n // CHUNK
    whole = pl.BlockSpec(memory_space=pltpu.VMEM)
    return pl.pallas_call(
        functools.partial(teacher_kernel, math.log2(math.e) * width**-0.5),
        out_shape=jax.ShapeDtypeStruct((blocks, rows, width), BF),
        in_specs=[pl.BlockSpec(memory_space=pltpu.SMEM), whole, whole, whole],
        out_specs=whole,
        scratch_shapes=[
            pltpu.VMEM((n, width), BF),
            pltpu.VMEM((n, width), BF),
            pltpu.VMEM((n, 2 * width), BF),
            pltpu.VMEM((n, width), BF),
            pltpu.VMEM((2, tiles, CHUNK, CHUNK), F32),
            pltpu.VMEM((2, CHUNK, n), BF),
        ],
        compiler_params=pltpu.CompilerParams(vmem_limit_bytes=48 * 2**20),
        cost_estimate=pl.CostEstimate(
            flops=2 * n * n * width, bytes_accessed=8 * n * width, transcendentals=n * n // 2
        ),
        name="teacher",
    )(place, q, k, v)


def twice(x, axis):
    return jnp.concatenate([x, x], axis=axis)


def student_kernel(
    loss_scale, place, q0, q1, k_ref, v_ref, t0, t1, wq, wk, o_ref, qs, ks, vs, ts, pqs, pks, zqs, zks, das, dds
):
    blocks, rows, width = k_ref.shape
    n = blocks * rows
    tiles = n // CHUNK
    heads = 2
    half = width // 2
    for p in range(blocks):
        b = place[p]
        span = pl.ds(p * rows, rows)
        qs[0, span, :] = q0[b]
        qs[1, span, :] = q1[b]
        ts[0, span, :] = t0[b]
        ts[1, span, :] = t1[b]
        ks[span, :] = k_ref[b]
        vs[span, :width] = v_ref[b]
    vs[:, width:] = jnp.ones((n, width), BF)
    mask = lower_mask()
    lanes = lax.broadcasted_iota(jnp.int32, (CHUNK, width), 1)
    left = lanes < half
    same = (lax.broadcasted_iota(jnp.int32, (2 * width, width), 0) // half % 2) == (
        lax.broadcasted_iota(jnp.int32, (2 * width, width), 1) // half
    )
    group = jnp.where(same, 1.0, 0.0).astype(BF)

    def halves_sum(x):
        return mm(jnp.concatenate(split(x), axis=1), group)

    def wide(w):
        return jnp.concatenate(split(jnp.concatenate([w, -w], axis=1)), axis=1)

    def features(x, w):
        both = mm(x, w)
        z = both[:, :width] + both[:, width:]
        top = jnp.max(jnp.where(left, z, -jnp.inf), axis=1, keepdims=True)
        other = jnp.max(jnp.where(left, -jnp.inf, z), axis=1, keepdims=True)
        e = jnp.exp(z - jnp.where(left, top, other))
        return jnp.concatenate(split(e / halves_sum(e)), axis=1)

    def back(feats, d):
        p = feats[:, :width].astype(F32) + feats[:, width:].astype(F32)
        x = p * d
        return jnp.concatenate(split(x - p * halves_sum(x)), axis=1)

    wqs = [wide(wq[h]) for h in range(heads)]
    wks = [wide(wk[h]) for h in range(heads)]
    states = [jnp.zeros((width, 2 * width), F32) for _ in range(heads)]
    for c in range(tiles):
        at = slice(c * CHUNK, (c + 1) * CHUNK)
        v1 = vs[at, :]
        for h in range(heads):
            pq = features(qs[h, at, :], wqs[h])
            pk = features(ks[at, :], wks[h])
            pqs[h, at, :] = pq
            pks[h, at, :] = pk
            pk_high = pk[:, :width]
            within = jnp.where(mask, mm(pq, twice(pk_high, 1), 1, 1), 0.0).astype(BF)
            state = states[h].astype(BF)
            both = mm(
                jnp.concatenate([within, pq], axis=1), jnp.concatenate([v1, state, state], axis=0)
            )
            inverse = 1.0 / both[:, width:]
            out = both[:, :width] * inverse
            g = (out - ts[h, at, :].astype(F32)) * (2.0 * loss_scale)
            dd = -jnp.sum(g * out, axis=1, keepdims=True) * inverse
            dd_high, dd_low = split(dd)
            dd_pair = jnp.where(
                lanes == 0, dd_high.astype(F32), jnp.where(lanes == 1, dd_low.astype(F32), 0.0)
            ).astype(BF)
            d = jnp.concatenate([(g * inverse).astype(BF), dd_pair], axis=1)
            da = jnp.where(mask, mm(d, v1, 1, 1), 0.0).astype(BF)
            das[h, c] = da
            dds[h, at, :] = d
            dp = mm(da, pk)
            dp = dp[:, :width] + dp[:, width:] + mm(d, state, 1, 1)
            zqs[h, at, :] = back(pq, dp)
            states[h] = states[h] + mm(pk_high, v1, 0, 0)
    sums = [jnp.zeros((width, 2 * width), F32) for _ in range(heads)]
    for c in reversed(range(tiles)):
        at = slice(c * CHUNK, (c + 1) * CHUNK)
        v1 = vs[at, :]
        for h in range(heads):
            pq = pqs[h, at, :]
            dp = mm(das[h, c], pq, 0, 0)
            dp = dp[:, :width] + dp[:, width:] + mm(v1, sums[h].astype(BF), 1, 1)
            zks[h, at, :] = back(pks[h, at, :], dp)
            sums[h] = sums[h] + mm(pq[:, :width], dds[h, at, :], 0, 0)
    for h in range(heads):
        gq = mm(qs[h], zqs[h], 0, 0)
        gk = mm(ks[...], zks[h], 0, 0)
        gq = gq[:, :width] + gq[:, width:]
        gk = gk[:, :width] + gk[:, width:]
        o_ref[h] = jnp.concatenate(
            [gq[:, :half] - gq[:, half:], gk[:, :half] - gk[:, half:]], axis=1
        )


def student(place, q0, q1, k, v, t0, t1, wq, wk, loss_scale):
    blocks, rows, width = k.shape
    n = blocks * rows
    tiles = n // CHUNK
    whole = pl.BlockSpec(memory_space=pltpu.VMEM)
    wide = pltpu.VMEM((2, n, 2 * width), BF)
    return pl.pallas_call(
        functools.partial(student_kernel, loss_scale),
        out_shape=jax.ShapeDtypeStruct((2, width, width), F32),
        in_specs=[pl.BlockSpec(memory_space=pltpu.SMEM)] + [whole] * 8,
        out_specs=whole,
        scratch_shapes=[
            pltpu.VMEM((2, n, width), BF),
            pltpu.VMEM((n, width), BF),
            pltpu.VMEM((n, 2 * width), BF),
            pltpu.VMEM((2, n, width), BF),
            wide,
            wide,
            wide,
            wide,
            pltpu.VMEM((2, tiles, CHUNK, CHUNK), BF),
            wide,
        ],
        compiler_params=pltpu.CompilerParams(vmem_limit_bytes=56 * 2**20),
        cost_estimate=pl.CostEstimate(
            flops=64 * n * width * CHUNK, bytes_accessed=12 * n * width, transcendentals=4 * n * width
        ),
        name="student",
    )(place, q0, q1, k, v, t0, t1, wq, wk)


def exchange(x, axis):
    return lax.all_to_all(x, axis, split_axis=0, concat_axis=0, tiled=True)


def sum_over(x, axis):
    size = lax.axis_size(axis)
    step = size // 2
    while step:
        x = x + lax.ppermute(x, axis, [(i, i ^ step) for i in range(size)])
        step //= 2
    return x


def on_device(queries, keys, values, block_order, query_maps, key_maps):
    rows = queries.shape[0]
    ctx = lax.axis_size("ctx")
    heads, width, half = query_maps.shape
    kv_heads = keys.shape[1] // width
    shared = ctx // kv_heads
    ids = jnp.arange(ctx, dtype=jnp.int32)
    place = jnp.sum(jnp.where(block_order[0][:, None] == ids[None, :], ids[:, None], 0), axis=0)

    def spread(x):
        x = x.reshape(rows, kv_heads, width).transpose(1, 0, 2)
        return jnp.repeat(x, shared, axis=0)

    by_head = queries.reshape(rows, ctx, heads, width).transpose(2, 1, 0, 3)
    first = exchange(jnp.concatenate([spread(keys), spread(values), by_head[0]], axis=2), "ctx")
    k, v, q0 = jnp.split(first, 3, axis=2)
    q1 = exchange(by_head[1], "ctx")
    t0 = teacher(place, q0, k, v)
    t1 = teacher(place, q1, k, v)
    back = exchange(jnp.concatenate([t0, t1], axis=2), "ctx")
    teacher_out = back.transpose(1, 0, 2).reshape(rows, ctx * heads * width)
    grads = student(place, q0, q1, k, v, t0, t1, query_maps, key_maps, 1.0 / lax.axis_size("dp"))
    grads = sum_over(grads, "dp")
    return teacher_out, grads[:, :, :half], grads[:, :, half:]


def solution(mesh):
    in_specs = (
        P(("dp", "ctx"), None),
        P(("dp", "ctx"), None),
        P(("dp", "ctx"), None),
        P("dp", None),
        P("ctx", None, None),
        P("ctx", None, None),
    )
    out_specs = (P(("dp", "ctx"), None), P("ctx", None, None), P("ctx", None, None))
    return jax.shard_map(
        on_device, mesh=mesh, in_specs=in_specs, out_specs=out_specs, check_vma=False
    )
```

```python
import functools
import math

import jax
import jax.numpy as jnp
from jax import lax
from jax.experimental import pallas as pl
from jax.experimental.pallas import tpu as pltpu
from jax.sharding import PartitionSpec as P

BF = jnp.bfloat16
F32 = jnp.float32
CHUNK = 256
STRIDE = 100
LEAD = 1


def mm(a, b, ca=1, cb=0):
    return lax.dot_general(a, b, (((ca,), (cb,)), ((), ())), preferred_element_type=F32)


def split(x):
    high = x.astype(BF)
    return high, (x - high.astype(F32)).astype(BF)


def join(*parts):
    return jnp.concatenate(parts, axis=1)


def lower_mask():
    rows = lax.broadcasted_iota(jnp.int32, (CHUNK, CHUNK), 0)
    cols = lax.broadcasted_iota(jnp.int32, (CHUNK, CHUNK), 1)
    return cols <= rows


def load(place, blocks, sems, parts):
    copies = []
    for a, part in enumerate(parts):
        for p in range(blocks):
            copy = pltpu.make_async_copy(*part(place[p], p), sems.at[a, p])
            copy.start()
            copies.append(copy)
    for copy in copies:
        copy.wait()


def key_value_parts(place, rows, blocks, width, own_ref, other_ref, kvs):
    core = place[blocks]

    def part(ref, side):
        def one(b, p):
            start = pl.multiple_of(p * 2 * rows + side * rows, 32)
            return ref.at[b, :, pl.ds(0, 2 * width)], kvs.at[pl.ds(start, rows), pl.ds(0, 2 * width)]

        return one

    return [part(own_ref, core), part(other_ref, 1 - core)]


def first_query_parts(rows, width, ref, target):
    def part(side):
        return lambda b, p: (
            ref.at[b, :, pl.ds((2 + side) * width, width)],
            target.at[pl.ds((2 * p + side) * rows, rows)],
        )

    return [part(0), part(1)]


def block_part(ref, lane, width, rows, target):
    return lambda b, p: (ref.at[b, :, pl.ds(lane, width)], target.at[pl.ds(p * rows, rows)])


def run(units):
    active = list(units)
    while active:
        active = [u for u in active if next(u, True) is None]


def staggered(units):
    active = []
    for unit in units:
        active = [u for u in active if next(u, True) is None]
        if next(unit, True) is None:
            active.append(unit)
    run(active)


def head_kernel(head, heads, scale, loss_scale, place, own_ref, other_ref, wq_ref, wk_ref, *refs):
    q_ref, gin_ref = (refs[0], refs[2]) if head else (own_ref, None)
    o_ref, g_ref, qs, kvs, ts, scores, probs, pqs, pks, zqs, zks, das, steps, maps, sems, out_sems, map_sems = refs[-17:]
    blocks, rows, _ = own_ref.shape
    n, width = qs.shape
    half = width // 2
    tiles = n // CHUNK
    parts = key_value_parts(place, rows, blocks, width, own_ref, other_ref, kvs)
    if head == 0:
        parts += first_query_parts(rows, width, q_ref, qs)
    else:
        parts.append(block_part(q_ref, 0, width, 2 * rows, qs))
        for h in range(head):
            g_ref[h] = gin_ref[h]
    kvs[:, 2 * width :] = jnp.ones((n, width), BF)
    map_copies = [
        pltpu.make_async_copy(ref.at[head], maps.at[i], map_sems.at[i])
        for i, ref in enumerate((wq_ref, wk_ref))
    ]
    for copy in map_copies:
        copy.start()
    load(place, blocks, sems, parts)
    for copy in map_copies:
        copy.wait()

    mask = lower_mask()
    lanes = lax.broadcasted_iota(jnp.int32, (CHUNK, width), 1)
    left = lanes < half
    square = (2 * width, 2 * width)
    group = jnp.where(
        lax.broadcasted_iota(jnp.int32, square, 0) // half
        == lax.broadcasted_iota(jnp.int32, square, 1) // half,
        1.0,
        0.0,
    ).astype(BF)
    tops = {}
    finished = set()
    active = []

    def first(i, j):
        s = mm(qs[pl.ds(i * CHUNK, CHUNK), :], kvs[pl.ds(j * CHUNK, CHUNK), :width], 1, 1)
        if i == j:
            s = jnp.where(mask, s, -1e30)
        scores[i % 2, j] = s
        top = functools.reduce(
            jnp.maximum, [s[:, g * width : (g + 1) * width] for g in range(CHUNK // width)]
        )
        tops[i] = top if j == 0 else jnp.maximum(tops[i], top)

    def second(i, j, peak):
        p = jnp.exp2((scores[i % 2, j] - peak) * scale)
        probs[i % 2, :, j * CHUNK : (j + 1) * CHUNK] = p.astype(BF)

    def finish(i):
        keys = (i + 1) * CHUNK
        both = mm(probs[i % 2, :, :keys], kvs[:keys, width:])
        ts[pl.ds(i * CHUNK, CHUNK), :] = (both[:, :width] / both[:, width:]).astype(BF)
        finished.add(i)

    def teach():
        for i in range(tiles + 1):
            if i > 0:
                peak = jnp.max(tops[i - 1], axis=1, keepdims=True)
            for j in range(i + 1):
                if i < tiles:
                    first(i, j)
                if i > 0 and j < i:
                    second(i - 1, j, peak)
                if j % STRIDE == STRIDE - 1:
                    yield
            if i > 0:
                finish(i - 1)
            yield

    def tall(w):
        return join(*split(jnp.concatenate([w, -w], axis=0)))

    def halves_sum(xs):
        if len(xs) == 1:
            return [mm(xs[0].astype(BF), group[:width, :width])]
        total = mm(join(*[x.astype(BF) for x in xs]), group)
        return [total[:, :width], total[:, width:]]

    def features(zs):
        tops = []
        for z in zs:
            top = jnp.max(jnp.where(left, z, -jnp.inf), axis=1, keepdims=True)
            other = jnp.max(jnp.where(left, -jnp.inf, z), axis=1, keepdims=True)
            tops.append(jnp.where(left, top, other))
        yield
        es = [jnp.exp(z - top) for z, top in zip(zs, tops)]
        totals = halves_sum(es)
        yield
        return [join(*split(e / total)) for e, total in zip(es, totals)]

    def back(feats, ds):
        ps = [f[:, :width].astype(F32) + f[:, width:].astype(F32) for f in feats]
        xs = [p * d for p, d in zip(ps, ds)]
        totals = halves_sum(xs)
        yield
        return [join(*split(x - p * total)) for x, p, total in zip(xs, ps, totals)]

    wq = tall(maps[0])
    wk = tall(maps[1])
    carry = [jnp.zeros((width, 2 * width), F32) for _ in range(2)]

    def ahead(c):
        at = slice(c * CHUNK, (c + 1) * CHUNK)
        q, k, v1 = qs[at, :], kvs[at, :width], kvs[at, width:]
        zs = [mm(join(q, q), wq, 1, 1), mm(join(k, k), wk, 1, 1)]
        yield
        pq, pk = yield from features(zs)
        pqs[at, :] = pq
        pks[at, :] = pk
        high = pk[:, :width]
        within = mm(pq, join(high, high), 1, 1)
        step = mm(high, v1, 0, 0)
        yield
        within = jnp.where(mask, within, 0.0).astype(BF)
        state = carry[0].astype(BF)
        carry[0] = carry[0] + step
        both = mm(join(within, pq), jnp.concatenate([v1, state, state], axis=0))
        yield
        inverse = 1.0 / both[:, width:]
        out = both[:, :width] * inverse
        while c not in finished:
            yield
        g = (out - ts[at, :].astype(F32)) * (2.0 * loss_scale)
        dd = jnp.sum(g * out, axis=1, keepdims=True) * -inverse
        yield
        dd_high, dd_low = split(dd)
        dd_pair = jnp.where(lanes == 0, dd_high, jnp.where(lanes == 1, dd_low, jnp.zeros_like(dd_low)))
        d = join((g * inverse).astype(BF), dd_pair)
        da = mm(d, v1, 1, 1)
        past = mm(d, state, 1, 1)
        steps[c] = mm(pq[:, :width], d, 0, 0)
        yield
        da = jnp.where(mask, da, 0.0).astype(BF)
        das[c] = da
        dp = mm(da, pk)
        yield
        dp = dp[:, :width] + dp[:, width:] + past
        (zqs[at, :],) = yield from back([pq], [dp])

    def behind(c):
        at = slice(c * CHUNK, (c + 1) * CHUNK)
        dp = mm(das[c], pqs[at, :], 0, 0)
        past = mm(kvs[at, width:], carry[1].astype(BF), 1, 1)
        carry[1] = carry[1] + steps[c]
        yield
        dp = dp[:, :width] + dp[:, width:] + past
        (zks[at, :],) = yield from back([pks[at, :]], [dp])

    def grad(row, x, z):
        g = mm(x, z, 0, 0)
        g = (g[:, :width] + g[:, width:]).T
        g_ref[head, pl.ds(row, half), :] = g[:half] - g[half:]

    lesson = teach()
    spawned = 0
    while len(finished) < tiles or active:
        before = len(finished)
        if len(finished) < tiles:
            next(lesson, None)
        active = [u for u in active if next(u, True) is None]
        while spawned < min(tiles, len(finished) + LEAD):
            unit = ahead(spawned)
            next(unit)
            active.append(unit)
            spawned += 1
    stores = []
    for p in range(blocks):
        store = pltpu.make_async_copy(
            ts.at[pl.ds(p * 2 * rows, 2 * rows)],
            o_ref.at[place[p], :, pl.ds(head * width, width)],
            out_sems.at[p],
        )
        store.start()
        stores.append(store)
    staggered([behind(c) for c in reversed(range(tiles))])
    grad(0, qs[...], zqs[...])
    grad(half, kvs[:, :width], zks[...])
    for store in stores:
        store.wait()


def one_head(head, place, own, other, wq, wk, loss_scale, *rest):
    blocks, rows, width = own.shape[0], own.shape[1], own.shape[2] // 4
    heads, half, _ = wq.shape
    n = 2 * blocks * rows
    tiles = n // CHUNK
    whole = pl.BlockSpec(memory_space=pltpu.VMEM)
    anywhere = pl.BlockSpec(memory_space=pl.ANY)
    hbm = pl.BlockSpec(memory_space=pltpu.HBM)
    specs = [pl.BlockSpec(memory_space=pltpu.SMEM), anywhere, anywhere, hbm, hbm]
    wide = pltpu.VMEM((n, 2 * width), BF)
    return pl.pallas_call(
        functools.partial(head_kernel, head, heads, math.log2(math.e) * width**-0.5, loss_scale),
        out_shape=(
            jax.ShapeDtypeStruct((blocks, 2 * rows, heads * width), BF),
            jax.ShapeDtypeStruct((heads, 2 * half, width), F32),
        ),
        in_specs=specs + [anywhere, hbm, whole][: len(rest)],
        out_specs=(hbm, whole),
        input_output_aliases={6: 0} if rest else {},
        scratch_shapes=[
            pltpu.VMEM((n, width), BF),
            pltpu.VMEM((n, 3 * width), BF),
            pltpu.VMEM((n, width), BF),
            pltpu.VMEM((2, tiles, CHUNK, CHUNK), F32),
            pltpu.VMEM((2, CHUNK, n), BF),
            wide,
            wide,
            wide,
            wide,
            pltpu.VMEM((tiles, CHUNK, CHUNK), BF),
            pltpu.VMEM((tiles, width, 2 * width), F32),
            pltpu.VMEM((2, half, width), F32),
            pltpu.SemaphoreType.DMA((4, blocks)),
            pltpu.SemaphoreType.DMA((blocks,)),
            pltpu.SemaphoreType.DMA((2,)),
        ],
        compiler_params=pltpu.CompilerParams(vmem_limit_bytes=40 * 2**20),
        cost_estimate=pl.CostEstimate(
            flops=2 * n * n * width + 32 * n * width * CHUNK,
            bytes_accessed=8 * n * width,
            transcendentals=n * n // 2 + 2 * n * width,
        ),
        name="one_head",
    )(place, own, other, wq, wk, *rest)


def pack_kernel(q_ref, k_ref, v_ref, x_ref, y_ref, sems):
    ctx, rows, lanes = x_ref.shape
    width = lanes // 4
    shared = ctx * width // k_ref.shape[1]
    copies = []

    def move(source, target):
        copy = pltpu.make_async_copy(source, target, sems.at[len(copies)])
        copy.start()
        copies.append(copy)

    for c in range(ctx):
        mine = pl.ds(c % 2 * rows, rows)
        kv = pl.ds(c // shared * width, width)
        move(k_ref.at[mine, kv], x_ref.at[c, :, pl.ds(0, width)])
        move(v_ref.at[mine, kv], x_ref.at[c, :, pl.ds(width, width)])
        for side in range(2):
            move(
                q_ref.at[pl.ds(side * rows, rows), pl.ds(2 * c * width, width)],
                x_ref.at[c, :, pl.ds((2 + side) * width, width)],
            )
        move(q_ref.at[:, pl.ds((2 * c + 1) * width, width)], y_ref.at[c])
    for copy in copies:
        copy.wait()


def pack(queries, keys, values, ctx, width):
    rows = queries.shape[0]
    whole = pl.BlockSpec(memory_space=pltpu.VMEM)
    hbm = pl.BlockSpec(memory_space=pltpu.HBM)
    return pl.pallas_call(
        pack_kernel,
        out_shape=(
            jax.ShapeDtypeStruct((ctx, rows // 2, 4 * width), BF),
            jax.ShapeDtypeStruct((ctx, rows, width), BF),
        ),
        in_specs=[hbm] * 3,
        out_specs=(whole, whole),
        scratch_shapes=[pltpu.SemaphoreType.DMA((5 * ctx,))],
        compiler_params=pltpu.CompilerParams(vmem_limit_bytes=16 * 2**20),
        name="pack",
    )(queries, keys, values)


def exchange(x, axis):
    return lax.all_to_all(x, axis, split_axis=0, concat_axis=0, tiled=True)


def sum_over(x, axis):
    size = lax.axis_size(axis)
    for step in (4, 2, 1, 8):
        x = x + lax.ppermute(x, axis, [(i, i ^ step) for i in range(size)])
    return x


def on_device(queries, keys, values, block_order, query_maps, key_maps):
    rows = queries.shape[0]
    ctx = lax.axis_size("ctx")
    heads, width, half = query_maps.shape
    ids = jnp.arange(ctx, dtype=jnp.int32)
    place = jnp.sum(jnp.where(block_order[0][:, None] == ids[None, :], ids[:, None], 0), axis=0)
    place = jnp.append(place, lax.axis_index("ctx") % 2)

    first, second = pack(queries, keys, values, ctx, width)
    own = exchange(first, "ctx")
    other = lax.ppermute(own, "ctx", [(i, i ^ 1) for i in range(ctx)])
    q1 = exchange(second, "ctx")
    maps = query_maps.transpose(0, 2, 1), key_maps.transpose(0, 2, 1)
    scale = 1.0 / lax.axis_size("dp")
    t, grads = one_head(0, place, own, other, *maps, scale)
    t, grads = one_head(1, place, own, other, *maps, scale, q1, t, grads)
    t, grads = lax.optimization_barrier((t, grads))
    teacher_out = exchange(t, "ctx").transpose(1, 0, 2).reshape(rows, ctx * heads * width)
    grads = sum_over(grads, "dp").transpose(0, 2, 1)
    return teacher_out, grads[:, :, :half], grads[:, :, half:]


def solution(mesh):
    in_specs = (
        P(("dp", "ctx"), None),
        P(("dp", "ctx"), None),
        P(("dp", "ctx"), None),
        P("dp", None),
        P("ctx", None, None),
        P("ctx", None, None),
    )
    out_specs = (P(("dp", "ctx"), None), P("ctx", None, None), P("ctx", None, None))
    return jax.shard_map(
        on_device, mesh=mesh, in_specs=in_specs, out_specs=out_specs, check_vma=False
    )
```

```python
import functools
import math

import jax
import jax.numpy as jnp
from jax import lax
from jax.experimental import pallas as pl
from jax.experimental.pallas import tpu as pltpu
from jax.sharding import PartitionSpec as P

BF = jnp.bfloat16
F32 = jnp.float32
CHUNK = 256
STRIDE = 100
LEAD = 1


def mm(a, b, ca=1, cb=0):
    return lax.dot_general(a, b, (((ca,), (cb,)), ((), ())), preferred_element_type=F32)


def split(x):
    high = x.astype(BF)
    return high, (x - high.astype(F32)).astype(BF)


def join(*parts):
    return jnp.concatenate(parts, axis=1)


def lower_mask():
    rows = lax.broadcasted_iota(jnp.int32, (CHUNK, CHUNK), 0)
    cols = lax.broadcasted_iota(jnp.int32, (CHUNK, CHUNK), 1)
    return cols <= rows


def in_order(place, own_ref, other_ref, q_ref, kvs, qs):
    blocks, rows, _ = own_ref.shape
    width = qs.shape[1]
    core = place[blocks]
    for p in range(blocks):
        b = place[p]
        for ref, side in ((own_ref, core), (other_ref, 1 - core)):
            start = pl.multiple_of(p * 2 * rows + side * rows, 32)
            kvs[pl.ds(start, rows), : 2 * width] = ref[b, :, : 2 * width]
        if q_ref is None:
            for side in range(2):
                qs[pl.ds((2 * p + side) * rows, rows), :] = own_ref[
                    b, :, (2 + side) * width : (3 + side) * width
                ]
        else:
            qs[pl.ds(p * 2 * rows, 2 * rows), :] = q_ref[b]


def run(units):
    active = list(units)
    while active:
        active = [u for u in active if next(u, True) is None]


def staggered(units):
    active = []
    for unit in units:
        active = [u for u in active if next(u, True) is None]
        if next(unit, True) is None:
            active.append(unit)
    run(active)


def head_kernel(head, heads, scale, loss_scale, place, own_ref, other_ref, wq_ref, wk_ref, *refs):
    q_ref, gin_ref = (refs[0], refs[2]) if head else (None, None)
    o_ref, g_ref, qs, kvs, ts, scores, probs, pqs, pks, zqs, zks, das, steps, maps, out_sems, map_sems = refs[-16:]
    blocks, rows, _ = own_ref.shape
    n, width = qs.shape
    half = width // 2
    tiles = n // CHUNK
    for h in range(head):
        g_ref[h] = gin_ref[h]
    map_copies = [
        pltpu.make_async_copy(ref.at[head], maps.at[i], map_sems.at[i])
        for i, ref in enumerate((wq_ref, wk_ref))
    ]
    for copy in map_copies:
        copy.start()
    kvs[:, 2 * width :] = jnp.ones((n, width), BF)
    in_order(place, own_ref, other_ref, q_ref, kvs, qs)
    for copy in map_copies:
        copy.wait()

    mask = lower_mask()
    lanes = lax.broadcasted_iota(jnp.int32, (CHUNK, width), 1)
    left = lanes < half
    tops = {}
    finished = set()
    active = []

    def first(i, j):
        s = mm(qs[pl.ds(i * CHUNK, CHUNK), :], kvs[pl.ds(j * CHUNK, CHUNK), :width], 1, 1)
        if i == j:
            s = jnp.where(mask, s, -1e30)
        scores[i % 2, j] = s
        top = functools.reduce(
            jnp.maximum, [s[:, g * width : (g + 1) * width] for g in range(CHUNK // width)]
        )
        tops[i] = top if j == 0 else jnp.maximum(tops[i], top)

    def second(i, j, peak):
        p = jnp.exp2((scores[i % 2, j] - peak) * scale)
        probs[i % 2, :, j * CHUNK : (j + 1) * CHUNK] = p.astype(BF)

    def finish(i):
        keys = (i + 1) * CHUNK
        both = mm(probs[i % 2, :, :keys], kvs[:keys, width:])
        ts[pl.ds(i * CHUNK, CHUNK), :] = (both[:, :width] / both[:, width:]).astype(BF)
        finished.add(i)

    def teach():
        for i in range(tiles + 1):
            if i > 0:
                peak = jnp.max(tops[i - 1], axis=1, keepdims=True)
            for j in range(i + 1):
                if i < tiles:
                    first(i, j)
                if i > 0 and j < i:
                    second(i - 1, j, peak)
                if j % STRIDE == STRIDE - 1:
                    yield
            if i > 0:
                finish(i - 1)
            yield

    def tall(w):
        return join(*split(jnp.concatenate([w, -w], axis=0)))

    def halves_sum(x):
        one = jnp.sum(jnp.where(left, x, 0.0), axis=1, keepdims=True)
        two = jnp.sum(jnp.where(left, 0.0, x), axis=1, keepdims=True)
        return jnp.where(left, one, two)

    def features(zs):
        tops = []
        for z in zs:
            top = jnp.max(jnp.where(left, z, -jnp.inf), axis=1, keepdims=True)
            other = jnp.max(jnp.where(left, -jnp.inf, z), axis=1, keepdims=True)
            tops.append(jnp.where(left, top, other))
        yield
        es = [jnp.exp(z - top) for z, top in zip(zs, tops)]
        totals = [halves_sum(e) for e in es]
        yield
        return [join(*split(e / total)) for e, total in zip(es, totals)]

    def back(feats, ds):
        ps = [f[:, :width].astype(F32) + f[:, width:].astype(F32) for f in feats]
        xs = [p * d for p, d in zip(ps, ds)]
        totals = [halves_sum(x) for x in xs]
        yield
        return [join(*split(x - p * total)) for x, p, total in zip(xs, ps, totals)]

    wq = tall(maps[0])
    wk = tall(maps[1])
    carry = [jnp.zeros((width, 2 * width), F32) for _ in range(2)]

    def ahead(c):
        at = slice(c * CHUNK, (c + 1) * CHUNK)
        q, k, v1 = qs[at, :], kvs[at, :width], kvs[at, width:]
        zs = [mm(join(q, q), wq, 1, 1), mm(join(k, k), wk, 1, 1)]
        yield
        pq, pk = yield from features(zs)
        pqs[at, :] = pq
        pks[at, :] = pk
        high = pk[:, :width]
        within = mm(pq, join(high, high), 1, 1)
        step = mm(high, v1, 0, 0)
        yield
        within = jnp.where(mask, within, 0.0).astype(BF)
        state = carry[0].astype(BF)
        carry[0] = carry[0] + step
        both = mm(join(within, pq), jnp.concatenate([v1, state, state], axis=0))
        yield
        inverse = 1.0 / both[:, width:]
        out = both[:, :width] * inverse
        while c not in finished:
            yield
        g = (out - ts[at, :].astype(F32)) * (2.0 * loss_scale)
        dd = jnp.sum(g * out, axis=1, keepdims=True) * -inverse
        yield
        dd_high, dd_low = split(dd)
        dd_pair = jnp.where(lanes == 0, dd_high, jnp.where(lanes == 1, dd_low, jnp.zeros_like(dd_low)))
        d = join((g * inverse).astype(BF), dd_pair)
        da = mm(d, v1, 1, 1)
        past = mm(d, state, 1, 1)
        steps[c] = mm(pq[:, :width], d, 0, 0)
        yield
        da = jnp.where(mask, da, 0.0).astype(BF)
        das[c] = da
        dp = mm(da, pk)
        yield
        dp = dp[:, :width] + dp[:, width:] + past
        (zqs[at, :],) = yield from back([pq], [dp])

    def behind(c):
        at = slice(c * CHUNK, (c + 1) * CHUNK)
        dp = mm(das[c], pqs[at, :], 0, 0)
        past = mm(kvs[at, width:], carry[1].astype(BF), 1, 1)
        carry[1] = carry[1] + steps[c]
        yield
        dp = dp[:, :width] + dp[:, width:] + past
        (zks[at, :],) = yield from back([pks[at, :]], [dp])

    def grad(row, x, z):
        g = mm(x, z, 0, 0)
        g = (g[:, :width] + g[:, width:]).T
        g_ref[head, pl.ds(row, half), :] = g[:half] - g[half:]

    lesson = teach()
    spawned = 0
    while len(finished) < tiles or active:
        before = len(finished)
        if len(finished) < tiles:
            next(lesson, None)
        active = [u for u in active if next(u, True) is None]
        while spawned < min(tiles, len(finished) + LEAD):
            unit = ahead(spawned)
            next(unit)
            active.append(unit)
            spawned += 1
    stores = []
    for p in range(blocks):
        store = pltpu.make_async_copy(
            ts.at[pl.ds(p * 2 * rows, 2 * rows)],
            o_ref.at[place[p], :, pl.ds(head * width, width)],
            out_sems.at[p],
        )
        store.start()
        stores.append(store)
    staggered([behind(c) for c in reversed(range(tiles))])
    grad(0, qs[...], zqs[...])
    grad(half, kvs[:, :width], zks[...])
    for store in stores:
        store.wait()


def one_head(head, place, own, other, wq, wk, loss_scale, *rest):
    blocks, rows, width = own.shape[0], own.shape[1], own.shape[2] // 4
    heads, half, _ = wq.shape
    n = 2 * blocks * rows
    tiles = n // CHUNK
    whole = pl.BlockSpec(memory_space=pltpu.VMEM)
    hbm = pl.BlockSpec(memory_space=pltpu.HBM)
    specs = [pl.BlockSpec(memory_space=pltpu.SMEM), whole, whole, hbm, hbm]
    wide = pltpu.VMEM((n, 2 * width), BF)
    return pl.pallas_call(
        functools.partial(head_kernel, head, heads, math.log2(math.e) * width**-0.5, loss_scale),
        out_shape=(
            jax.ShapeDtypeStruct((blocks, 2 * rows, heads * width), BF),
            jax.ShapeDtypeStruct((heads, 2 * half, width), F32),
        ),
        in_specs=specs + [whole, hbm, whole][: len(rest)],
        out_specs=(hbm, whole),
        input_output_aliases={6: 0} if rest else {},
        scratch_shapes=[
            pltpu.VMEM((n, width), BF),
            pltpu.VMEM((n, 3 * width), BF),
            pltpu.VMEM((n, width), BF),
            pltpu.VMEM((2, tiles, CHUNK, CHUNK), F32),
            pltpu.VMEM((2, CHUNK, n), BF),
            wide,
            wide,
            wide,
            wide,
            pltpu.VMEM((tiles, CHUNK, CHUNK), BF),
            pltpu.VMEM((tiles, width, 2 * width), F32),
            pltpu.VMEM((2, half, width), F32),
            pltpu.SemaphoreType.DMA((blocks,)),
            pltpu.SemaphoreType.DMA((2,)),
        ],
        compiler_params=pltpu.CompilerParams(vmem_limit_bytes=40 * 2**20),
        cost_estimate=pl.CostEstimate(
            flops=2 * n * n * width + 32 * n * width * CHUNK,
            bytes_accessed=8 * n * width,
            transcendentals=n * n // 2 + 2 * n * width,
        ),
        name="one_head",
    )(place, own, other, wq, wk, *rest)


def pack_kernel(q_ref, k_ref, v_ref, x_ref, y_ref, sems):
    ctx, rows, lanes = x_ref.shape
    width = lanes // 4
    shared = ctx * width // k_ref.shape[1]
    copies = []

    def move(source, target):
        copy = pltpu.make_async_copy(source, target, sems.at[len(copies)])
        copy.start()
        copies.append(copy)

    for c in range(ctx):
        mine = pl.ds(c % 2 * rows, rows)
        kv = pl.ds(c // shared * width, width)
        move(k_ref.at[mine, kv], x_ref.at[c, :, pl.ds(0, width)])
        move(v_ref.at[mine, kv], x_ref.at[c, :, pl.ds(width, width)])
        for side in range(2):
            move(
                q_ref.at[pl.ds(side * rows, rows), pl.ds(2 * c * width, width)],
                x_ref.at[c, :, pl.ds((2 + side) * width, width)],
            )
        move(q_ref.at[:, pl.ds((2 * c + 1) * width, width)], y_ref.at[c])
    for copy in copies:
        copy.wait()


def pack(queries, keys, values, ctx, width):
    rows = queries.shape[0]
    whole = pl.BlockSpec(memory_space=pltpu.VMEM)
    hbm = pl.BlockSpec(memory_space=pltpu.HBM)
    return pl.pallas_call(
        pack_kernel,
        out_shape=(
            jax.ShapeDtypeStruct((ctx, rows // 2, 4 * width), BF),
            jax.ShapeDtypeStruct((ctx, rows, width), BF),
        ),
        in_specs=[hbm] * 3,
        out_specs=(whole, whole),
        scratch_shapes=[pltpu.SemaphoreType.DMA((5 * ctx,))],
        compiler_params=pltpu.CompilerParams(vmem_limit_bytes=60 * 2**20),
        name="pack",
    )(queries, keys, values)


def exchange(x, axis):
    return lax.all_to_all(x, axis, split_axis=0, concat_axis=0, tiled=True)


def add_from(x, axis, step):
    size = lax.axis_size(axis)
    return x + lax.ppermute(x, axis, [(i, i ^ step) for i in range(size)])


def on_device(queries, keys, values, block_order, query_maps, key_maps):
    rows = queries.shape[0]
    ctx = lax.axis_size("ctx")
    heads, width, half = query_maps.shape
    ids = jnp.arange(ctx, dtype=jnp.int32)
    place = jnp.sum(jnp.where(block_order[0][:, None] == ids[None, :], ids[:, None], 0), axis=0)
    place = jnp.append(place, lax.axis_index("ctx") % 2)

    first, second = pack(queries, keys, values, ctx, width)
    own = exchange(first, "ctx")
    other = lax.ppermute(own, "ctx", [(i, i ^ 1) for i in range(ctx)])
    q1 = exchange(second, "ctx")
    maps = query_maps.transpose(0, 2, 1), key_maps.transpose(0, 2, 1)
    scale = 1.0 / lax.axis_size("dp")
    t, grads = one_head(0, place, own, other, *maps, scale)
    t, grads = one_head(1, place, own, other, *maps, scale, q1, t, grads)
    t, grads = lax.optimization_barrier((t, grads))
    teacher_out = exchange(t, "ctx").transpose(1, 0, 2).reshape(rows, ctx * heads * width)
    for step in (4, 2, 1, 8):
        grads = add_from(grads, "dp", step)
    grads = grads.transpose(0, 2, 1)
    return teacher_out, grads[:, :, :half], grads[:, :, half:]


def solution(mesh):
    in_specs = (
        P(("dp", "ctx"), None),
        P(("dp", "ctx"), None),
        P(("dp", "ctx"), None),
        P("dp", None),
        P("ctx", None, None),
        P("ctx", None, None),
    )
    out_specs = (P(("dp", "ctx"), None), P("ctx", None, None), P("ctx", None, None))
    return jax.shard_map(
        on_device, mesh=mesh, in_specs=in_specs, out_specs=out_specs, check_vma=False
    )
```

```python
import functools
import math

import jax
import jax.numpy as jnp
from jax import lax
from jax.experimental import pallas as pl
from jax.experimental.pallas import tpu as pltpu
from jax.sharding import PartitionSpec as P

BF = jnp.bfloat16
F32 = jnp.float32
CHUNK = 256
STRIDE = 100
LEAD = 1


def mm(a, b, ca=1, cb=0):
    return lax.dot_general(a, b, (((ca,), (cb,)), ((), ())), preferred_element_type=F32)


def split(x):
    high = x.astype(BF)
    return high, (x - high.astype(F32)).astype(BF)


def join(*parts):
    return jnp.concatenate(parts, axis=1)


def lower_mask():
    rows = lax.broadcasted_iota(jnp.int32, (CHUNK, CHUNK), 0)
    cols = lax.broadcasted_iota(jnp.int32, (CHUNK, CHUNK), 1)
    return cols <= rows


def in_order(place, own_ref, other_ref, q_ref, kvs, qs):
    blocks, rows, _ = own_ref.shape
    width = qs.shape[1]
    core = place[blocks]
    for p in range(blocks):
        b = place[p]
        for ref, side in ((own_ref, core), (other_ref, 1 - core)):
            start = pl.multiple_of(p * 2 * rows + side * rows, 32)
            kvs[pl.ds(start, rows), : 2 * width] = ref[b, :, : 2 * width]
        if q_ref is None:
            for side in range(2):
                qs[pl.ds((2 * p + side) * rows, rows), :] = own_ref[
                    b, :, (2 + side) * width : (3 + side) * width
                ]
        else:
            qs[pl.ds(p * 2 * rows, 2 * rows), :] = q_ref[b]


def run(units):
    active = list(units)
    while active:
        active = [u for u in active if next(u, True) is None]


def staggered(units):
    active = []
    for unit in units:
        active = [u for u in active if next(u, True) is None]
        if next(unit, True) is None:
            active.append(unit)
    run(active)


def head_kernel(head, heads, scale, loss_scale, place, own_ref, other_ref, wq_ref, wk_ref, *refs):
    q_ref, gin_ref = (refs[0], refs[2]) if head else (None, None)
    o_ref, g_ref, qs, kvs, ts, scores, probs, pqs, pks, zqs, zks, das, steps, maps, out_sems, map_sems = refs[-16:]
    blocks, rows, _ = own_ref.shape
    n, width = qs.shape
    half = width // 2
    tiles = n // CHUNK
    for h in range(head):
        g_ref[h] = gin_ref[h]
    map_copies = [
        pltpu.make_async_copy(ref.at[head], maps.at[i], map_sems.at[i])
        for i, ref in enumerate((wq_ref, wk_ref))
    ]
    for copy in map_copies:
        copy.start()
    kvs[:, 2 * width :] = jnp.ones((n, width), BF)
    in_order(place, own_ref, other_ref, q_ref, kvs, qs)
    for copy in map_copies:
        copy.wait()

    mask = lower_mask()
    lanes = lax.broadcasted_iota(jnp.int32, (CHUNK, width), 1)
    left = lanes < half
    tops = {}
    finished = set()
    active = []

    def first(i, j):
        s = mm(qs[pl.ds(i * CHUNK, CHUNK), :], kvs[pl.ds(j * CHUNK, CHUNK), :width], 1, 1)
        if i == j:
            s = jnp.where(mask, s, -1e30)
        scores[i % 2, j] = s
        top = functools.reduce(
            jnp.maximum, [s[:, g * width : (g + 1) * width] for g in range(CHUNK // width)]
        )
        tops[i] = top if j == 0 else jnp.maximum(tops[i], top)

    def second(i, j, peak):
        p = jnp.exp2((scores[i % 2, j] - peak) * scale)
        probs[i % 2, :, j * CHUNK : (j + 1) * CHUNK] = p.astype(BF)

    def finish(i):
        keys = (i + 1) * CHUNK
        both = mm(probs[i % 2, :, :keys], kvs[:keys, width:])
        ts[pl.ds(i * CHUNK, CHUNK), :] = (both[:, :width] / both[:, width:]).astype(BF)
        finished.add(i)

    def teach():
        for i in range(tiles + 1):
            if i > 0:
                peak = jnp.max(tops[i - 1], axis=1, keepdims=True)
            for j in range(i + 1):
                if i < tiles:
                    first(i, j)
                if i > 0 and j < i:
                    second(i - 1, j, peak)
                if j % STRIDE == STRIDE - 1:
                    yield
            if i > 0:
                finish(i - 1)
            yield

    def tall(w):
        return join(*split(jnp.concatenate([w, -w], axis=0)))

    def halves_sum(x):
        one = jnp.sum(jnp.where(left, x, 0.0), axis=1, keepdims=True)
        two = jnp.sum(jnp.where(left, 0.0, x), axis=1, keepdims=True)
        return jnp.where(left, one, two)

    def features(zs):
        tops = []
        for z in zs:
            top = jnp.max(jnp.where(left, z, -jnp.inf), axis=1, keepdims=True)
            other = jnp.max(jnp.where(left, -jnp.inf, z), axis=1, keepdims=True)
            tops.append(jnp.where(left, top, other))
        yield
        es = [jnp.exp(z - top) for z, top in zip(zs, tops)]
        totals = [halves_sum(e) for e in es]
        yield
        return [join(*split(e / total)) for e, total in zip(es, totals)]

    def back(feats, ds):
        ps = [f[:, :width].astype(F32) + f[:, width:].astype(F32) for f in feats]
        xs = [p * d for p, d in zip(ps, ds)]
        totals = [halves_sum(x) for x in xs]
        yield
        return [join(*split(x - p * total)) for x, p, total in zip(xs, ps, totals)]

    wq = tall(maps[0])
    wk = tall(maps[1])
    carry = [jnp.zeros((width, 2 * width), F32) for _ in range(2)]

    def ahead(c):
        at = slice(c * CHUNK, (c + 1) * CHUNK)
        q, k, v1 = qs[at, :], kvs[at, :width], kvs[at, width:]
        zs = [mm(join(q, q), wq, 1, 1), mm(join(k, k), wk, 1, 1)]
        yield
        pq, pk = yield from features(zs)
        pqs[at, :] = pq
        pks[at, :] = pk
        high = pk[:, :width]
        within = mm(pq, join(high, high), 1, 1)
        step = mm(high, v1, 0, 0)
        yield
        within = jnp.where(mask, within, 0.0).astype(BF)
        state = carry[0].astype(BF)
        carry[0] = carry[0] + step
        both = mm(join(within, pq), jnp.concatenate([v1, state, state], axis=0))
        yield
        inverse = 1.0 / both[:, width:]
        out = both[:, :width] * inverse
        while c not in finished:
            yield
        g = (out - ts[at, :].astype(F32)) * (2.0 * loss_scale)
        dd = jnp.sum(g * out, axis=1, keepdims=True) * -inverse
        yield
        dd_high, dd_low = split(dd)
        dd_pair = jnp.where(lanes == 0, dd_high, jnp.where(lanes == 1, dd_low, jnp.zeros_like(dd_low)))
        d = join((g * inverse).astype(BF), dd_pair)
        da = mm(d, v1, 1, 1)
        past = mm(d, state, 1, 1)
        steps[c] = mm(pq[:, :width], d, 0, 0)
        yield
        da = jnp.where(mask, da, 0.0).astype(BF)
        das[c] = da
        dp = mm(da, pk)
        yield
        dp = dp[:, :width] + dp[:, width:] + past
        (zqs[at, :],) = yield from back([pq], [dp])

    def behind(c):
        at = slice(c * CHUNK, (c + 1) * CHUNK)
        dp = mm(das[c], pqs[at, :], 0, 0)
        past = mm(kvs[at, width:], carry[1].astype(BF), 1, 1)
        carry[1] = carry[1] + steps[c]
        yield
        dp = dp[:, :width] + dp[:, width:] + past
        (zks[at, :],) = yield from back([pks[at, :]], [dp])

    def grad(row, x, z):
        g = mm(x, z, 0, 0)
        g = (g[:, :width] + g[:, width:]).T
        g_ref[head, pl.ds(row, half), :] = g[:half] - g[half:]

    lesson = teach()
    spawned = 0
    while len(finished) < tiles or active:
        before = len(finished)
        if len(finished) < tiles:
            next(lesson, None)
        active = [u for u in active if next(u, True) is None]
        while spawned < min(tiles, len(finished) + LEAD):
            unit = ahead(spawned)
            next(unit)
            active.append(unit)
            spawned += 1
    stores = []
    for p in range(blocks):
        store = pltpu.make_async_copy(
            ts.at[pl.ds(p * 2 * rows, 2 * rows)],
            o_ref.at[place[p], :, pl.ds(head * width, width)],
            out_sems.at[p],
        )
        store.start()
        stores.append(store)
    staggered([behind(c) for c in reversed(range(tiles))])
    grad(0, qs[...], zqs[...])
    grad(half, kvs[:, :width], zks[...])
    for store in stores:
        store.wait()


def one_head(head, place, own, other, wq, wk, loss_scale, *rest):
    blocks, rows, width = own.shape[0], own.shape[1], own.shape[2] // 4
    heads, half, _ = wq.shape
    n = 2 * blocks * rows
    tiles = n // CHUNK
    whole = pl.BlockSpec(memory_space=pltpu.VMEM)
    hbm = pl.BlockSpec(memory_space=pltpu.HBM)
    specs = [pl.BlockSpec(memory_space=pltpu.SMEM), whole, whole, hbm, hbm]
    wide = pltpu.VMEM((n, 2 * width), BF)
    return pl.pallas_call(
        functools.partial(head_kernel, head, heads, math.log2(math.e) * width**-0.5, loss_scale),
        out_shape=(
            jax.ShapeDtypeStruct((blocks, 2 * rows, heads * width), BF),
            jax.ShapeDtypeStruct((heads, 2 * half, width), F32),
        ),
        in_specs=specs + [whole, hbm, whole][: len(rest)],
        out_specs=(hbm, whole),
        input_output_aliases={6: 0} if rest else {},
        scratch_shapes=[
            pltpu.VMEM((n, width), BF),
            pltpu.VMEM((n, 3 * width), BF),
            pltpu.VMEM((n, width), BF),
            pltpu.VMEM((2, tiles, CHUNK, CHUNK), F32),
            pltpu.VMEM((2, CHUNK, n), BF),
            wide,
            wide,
            wide,
            wide,
            pltpu.VMEM((tiles, CHUNK, CHUNK), BF),
            pltpu.VMEM((tiles, width, 2 * width), F32),
            pltpu.VMEM((2, half, width), F32),
            pltpu.SemaphoreType.DMA((blocks,)),
            pltpu.SemaphoreType.DMA((2,)),
        ],
        compiler_params=pltpu.CompilerParams(vmem_limit_bytes=40 * 2**20),
        cost_estimate=pl.CostEstimate(
            flops=2 * n * n * width + 32 * n * width * CHUNK,
            bytes_accessed=8 * n * width,
            transcendentals=n * n // 2 + 2 * n * width,
        ),
        name="one_head",
    )(place, own, other, wq, wk, *rest)


def pack_kernel(q_ref, k_ref, v_ref, x_ref, y_ref, xs, ys, sems, out_sems):
    ctx, rows, lanes = xs.shape
    width = lanes // 4
    shared = ctx * width // k_ref.shape[1]
    copies = [[] for _ in range(ctx)]

    def move(c, source, target):
        copy = pltpu.make_async_copy(source, target, sems.at[c, len(copies[c])])
        copy.start()
        copies[c].append(copy)

    for c in range(ctx):
        mine = pl.ds(c % 2 * rows, rows)
        kv = pl.ds(c // shared * width, width)
        move(c, k_ref.at[mine, kv], xs.at[c, :, pl.ds(0, width)])
        move(c, v_ref.at[mine, kv], xs.at[c, :, pl.ds(width, width)])
        for side in range(2):
            move(
                c,
                q_ref.at[pl.ds(side * rows, rows), pl.ds(2 * c * width, width)],
                xs.at[c, :, pl.ds((2 + side) * width, width)],
            )
        move(c, q_ref.at[:, pl.ds((2 * c + 1) * width, width)], ys.at[c])
    stores = []
    for c in range(ctx):
        for copy in copies[c]:
            copy.wait()
        for i, (source, target) in enumerate(((xs, x_ref), (ys, y_ref))):
            store = pltpu.make_async_copy(source.at[c], target.at[c], out_sems.at[c, i])
            store.start()
            stores.append(store)
    for store in stores:
        store.wait()


def pack(queries, keys, values, ctx, width):
    rows = queries.shape[0]
    hbm = pl.BlockSpec(memory_space=pltpu.HBM)
    first, second = (ctx, rows // 2, 4 * width), (ctx, rows, width)
    return pl.pallas_call(
        pack_kernel,
        out_shape=(jax.ShapeDtypeStruct(first, BF), jax.ShapeDtypeStruct(second, BF)),
        in_specs=[hbm] * 3,
        out_specs=(hbm, hbm),
        scratch_shapes=[
            pltpu.VMEM(first, BF),
            pltpu.VMEM(second, BF),
            pltpu.SemaphoreType.DMA((ctx, 5)),
            pltpu.SemaphoreType.DMA((ctx, 2)),
        ],
        compiler_params=pltpu.CompilerParams(vmem_limit_bytes=60 * 2**20),
        name="pack",
    )(queries, keys, values)


def exchange(x, axis):
    return lax.all_to_all(x, axis, split_axis=0, concat_axis=0, tiled=True)


def add_from(x, axis, step):
    size = lax.axis_size(axis)
    return x + lax.ppermute(x, axis, [(i, i ^ step) for i in range(size)])


def on_device(queries, keys, values, block_order, query_maps, key_maps):
    rows = queries.shape[0]
    ctx = lax.axis_size("ctx")
    heads, width, half = query_maps.shape
    ids = jnp.arange(ctx, dtype=jnp.int32)
    place = jnp.sum(jnp.where(block_order[0][:, None] == ids[None, :], ids[:, None], 0), axis=0)
    place = jnp.append(place, lax.axis_index("ctx") % 2)

    first, second = pack(queries, keys, values, ctx, width)
    own = exchange(first, "ctx")
    other = lax.ppermute(own, "ctx", [(i, i ^ 1) for i in range(ctx)])
    q1 = exchange(second, "ctx")
    maps = query_maps.transpose(0, 2, 1), key_maps.transpose(0, 2, 1)
    scale = 1.0 / lax.axis_size("dp")
    t, grads = one_head(0, place, own, other, *maps, scale)
    t, grads = one_head(1, place, own, other, *maps, scale, q1, t, grads)
    t, grads = lax.optimization_barrier((t, grads))
    teacher_out = exchange(t, "ctx").transpose(1, 0, 2).reshape(rows, ctx * heads * width)
    for step in (4, 2, 1, 8):
        grads = add_from(grads, "dp", step)
    grads = grads.transpose(0, 2, 1)
    return teacher_out, grads[:, :, :half], grads[:, :, half:]


def solution(mesh):
    in_specs = (
        P(("dp", "ctx"), None),
        P(("dp", "ctx"), None),
        P(("dp", "ctx"), None),
        P("dp", None),
        P("ctx", None, None),
        P("ctx", None, None),
    )
    out_specs = (P(("dp", "ctx"), None), P("ctx", None, None), P("ctx", None, None))
    return jax.shard_map(
        on_device, mesh=mesh, in_specs=in_specs, out_specs=out_specs, check_vma=False
    )
```
